32 devices in a mesh: row: 8 (over z, y), col: 4 (over x, core).
Axes of the slice: x: 2, y: 2, z: 4, core: 2. Of those that a mesh axis runs over, the one named last changes fastest.
Arguments:
- features: bfloat16 [4096, 1024], P(('row', 'col')), may hold values from -12 to 12
- tile_values: bfloat16 [8, 4, 24, 128, 128], P('row', 'col'), as said below
- tile_rows: int32 [8, 4, 24], P('row', 'col'), may hold values from 0 to 3
- tile_cols: int32 [8, 4, 24], P('row', 'col'), may hold values from 0 to 7
- tile_count: int32 [8, 4], P('row', 'col'), may hold values from 3 to 24, as said below
Outputs:
- smoothed: bfloat16 [4096, 1024], P(('row', 'col'))
The draws below stay inside these ranges and needn't reach their ends.
Inputs may be any that keep to these rules, and one draw needn't show every extreme that they name: `tile_count`: live slots of one device sit at distinct tile positions; in every grid row exactly one device has all 24 slots live. `tile_values`: edge weights are zero or positive.
All inputs are finite; a program needn't handle non-finite values.
Results may differ from the reference program's by a relative error of at most 0.0075.
Values may be sent and summed in bfloat16 or wider, within the bound.
A program may use at most 64 MiB of HBM per device.

```python
import math
import jax
import jax.numpy as jnp
from jax import lax

F = 1024
BT = 128
SH = 128
ITERS = 2
RT = 4
CT = 8
TILE_CAP = 24
AUTHORS = 4096
N_ROW = 8
N_COL = 4


def tile_layout(key):
    count_key = jax.random.fold_in(key, 101)
    heavy_key = jax.random.fold_in(key, 202)
    place_key = jax.random.fold_in(key, 303)
    counts = jax.random.randint(count_key, (N_ROW, N_COL), TILE_CAP // 8, TILE_CAP // 3 + 1)
    heavy = jax.random.randint(heavy_key, (N_ROW, 1), 0, N_COL)
    counts = jnp.where(jnp.arange(N_COL)[None, :] == heavy, TILE_CAP, counts).astype(jnp.int32)
    device_keys = jax.random.split(place_key, N_ROW * N_COL)
    places = jax.vmap(lambda one_key: jax.random.permutation(one_key, RT * CT)[:TILE_CAP])(device_keys)
    places = places.reshape(N_ROW, N_COL, TILE_CAP).astype(jnp.int32)
    return (counts, (places // CT).astype(jnp.int32), (places % CT).astype(jnp.int32))


def draw_tile_count(key, part):
    return tile_layout(key)[0]


def draw_tile_rows(key, part):
    return tile_layout(key)[1]


def draw_tile_cols(key, part):
    return tile_layout(key)[2]


def draw_tile_values(key, part):
    shape = (N_ROW, N_COL, TILE_CAP, BT, BT)
    mask_key = jax.random.fold_in(key, 404)
    size_key = jax.random.fold_in(key, 505)
    present = (jax.random.randint(mask_key, shape, 0, 3) == 0).astype(jnp.float32)
    magnitude = jnp.exp(jax.random.uniform(size_key, shape, jnp.float32, math.log(0.01), 0.0))
    return (present * magnitude).astype(jnp.bfloat16)


def block_levels(own_key, extent, cuts, least, top_value):
    level, own = 1.0, jax.random.fold_in(own_key, 6)
    for position, blocks in cuts:
        steps = jnp.exp(jax.random.uniform(jax.random.fold_in(own, position), (blocks,), jnp.float32, least / len(cuts), top_value / len(cuts)))
        level = level * jnp.repeat(steps, extent[position] // blocks).reshape([-1 if axis == position else 1 for axis in range(len(extent))])
    return level


def noise(key, extent, scale, bound, cuts=(), held_as=jnp.bfloat16):
    entries = jax.random.normal(key, extent, jnp.float32) * scale
    if len(cuts) > 0:
        entries = block_levels(key, extent, cuts, -0.22, 0.18) * entries
    return jnp.clip(entries, min=-bound, max=bound).astype(held_as)


def setup_inputs(seed: int = 0) -> dict:
    key_of = jax.random.split(jax.random.key(seed), 6)
    return {
        "features": noise(key_of[0], (AUTHORS, F), 3.0, 12.0, ((0, 32),)),
        "tile_values": draw_tile_values(jax.random.fold_in(key_of[5], 71), 0),
        "tile_rows": draw_tile_rows(jax.random.fold_in(key_of[5], 71), 0),
        "tile_cols": draw_tile_cols(jax.random.fold_in(key_of[5], 71), 0),
        "tile_count": draw_tile_count(jax.random.fold_in(key_of[5], 71), 0),
    }


retain_share = 0.9
restart_share = 0.1


def device_partial(column_blocks, tile_set, row_ids, col_ids, live_count):
    is_live = jnp.arange(TILE_CAP) < live_count
    chosen = jnp.take(column_blocks, col_ids, axis=0).astype(jnp.float32)
    product = jnp.einsum("tij,tjf->tif", tile_set.astype(jnp.float32), chosen, precision=lax.Precision.HIGHEST)
    row_hot = ((row_ids[None, :] == jnp.arange(RT)[:, None]) & is_live[None, :]).astype(jnp.float32)
    spread = jnp.einsum("rt,tif->rif", row_hot, product, precision=lax.Precision.HIGHEST)
    return spread.reshape(RT * BT, F)


def device_degree(tile_set, row_ids, live_count):
    is_live = jnp.arange(TILE_CAP) < live_count
    row_sums = jnp.sum(tile_set.astype(jnp.float32), axis=2)
    row_hot = ((row_ids[None, :] == jnp.arange(RT)[:, None]) & is_live[None, :]).astype(jnp.float32)
    return jnp.einsum("rt,ti->ri", row_hot, row_sums, precision=lax.Precision.HIGHEST).reshape(RT * BT)


def reference(features, tile_values, tile_rows, tile_cols, tile_count):
    def degree_row(row_index):
        def one_device(col_index):
            return device_degree(tile_values[row_index, col_index], tile_rows[row_index, col_index], tile_count[row_index, col_index])
        return jnp.sum(lax.map(one_device, jnp.arange(N_COL)), axis=0)

    degree = 1.0 + lax.map(degree_row, jnp.arange(N_ROW)).reshape(-1)
    source = features.astype(jnp.float32)
    current = features
    for iteration in range(ITERS):
        grouped = current.reshape(N_ROW, N_COL, SH, F)

        def row_total(row_index):
            def one_device(col_index):
                column_blocks = grouped[:, col_index].reshape(CT, BT, F)
                partial_value = device_partial(column_blocks, tile_values[row_index, col_index], tile_rows[row_index, col_index], tile_cols[row_index, col_index], tile_count[row_index, col_index])
                return partial_value.astype(jnp.bfloat16)
            pieces = lax.map(one_device, jnp.arange(N_COL))
            return jnp.sum(pieces.astype(jnp.float32), axis=0)

        summed = lax.map(row_total, jnp.arange(N_ROW)).reshape(-1, F)
        current = ((retain_share * (summed + current.astype(jnp.float32))) / degree[:, None] + restart_share * source).astype(jnp.bfloat16)
    return current
```

```python
import functools
import math

import jax
import jax.numpy as jnp
from jax import lax
from jax.experimental import pallas as pl
from jax.experimental.pallas import tpu as pltpu
from jax.sharding import PartitionSpec as P

ITERS = 2
RETAIN = 0.9
RESTART = 0.1
MESH = pl.DeviceIdType.MESH
F32 = jnp.float32
BF16 = jnp.bfloat16


def kernel(
    nz, ny, nx, chunk,
    feat_ref, tiles_ref, rows_ref, cols_ref, count_ref,
    out_ref,
    pos, wout, wd, dsend, drecv, scale,
    zbuf, csend, crecv, keep_c, ysend, yrecv, keep_y, xsend, xrecv, keep_x,
    w_ss, w_rs, d_ss, d_rs, z_ss, z_rs, c_ss, c_rs, y_ss, y_rs, x_ss, x_rs,
):
    row, col = lax.axis_index("row"), lax.axis_index("col")
    z, y, x, core = row // ny, row % ny, col // 2, col % 2
    ncol = nx * 2
    shard, width = feat_ref.shape
    cap, bt = tiles_ref.shape[0], tiles_ref.shape[1]
    chunks = width // chunk
    jobs = ITERS * chunks
    col_tiles = nz * ny

    def z_peer(d):
        return (lax.rem(z + d, nz) * ny + y, col)

    def y_peer(d):
        return (z * ny + lax.rem(y + d, ny), col)

    def col_peer(d):
        return (row, lax.rem(col + d, ncol))

    def x_peer(d):
        return (row, lax.rem(x + d, nx) * 2 + core)

    sibling = (row, x * 2 + 1 - core)

    def remote(src, dst, ss, rs, device):
        return pltpu.make_async_remote_copy(
            src_ref=src, dst_ref=dst, send_sem=ss, recv_sem=rs, device_id=device, device_id_type=MESH
        )

    def z_copy(it, k, d, owner):
        j = it * chunks + k
        return remote(
            zbuf.at[it, k, owner], zbuf.at[it, k, owner], z_ss.at[j, d - 1], z_rs.at[j, d - 1], z_peer(d)
        )

    def c_copy(j):
        return remote(csend.at[j], crecv.at[j], c_ss.at[j], c_rs.at[j], sibling)

    def y_copy(j, d):
        return remote(ysend.at[j, d - 1], yrecv.at[j, d - 1], y_ss.at[j, d - 1], y_rs.at[j, d - 1], y_peer(d))

    def x_copy(j, d):
        return remote(xsend.at[j, d - 1], xrecv.at[j, d - 1], x_ss.at[j, d - 1], x_rs.at[j, d - 1], x_peer(d))

    def w_copy(d, slot):
        return remote(wout.at[lax.rem(y + d, ny)], wd.at[slot], w_ss.at[d - 1], w_rs.at[d - 1], y_peer(d))

    def d_copy(d):
        return remote(dsend.at[lax.rem(col + d, ncol)], drecv.at[d - 1], d_ss.at[d - 1], d_rs.at[d - 1], col_peer(d))

    barrier = pltpu.get_barrier_semaphore()
    peers = (
        [z_peer(d) for d in range(1, nz)]
        + [y_peer(d) for d in range(1, ny)]
        + [col_peer(d) for d in range(1, ncol)]
    )
    for device in peers:
        pl.semaphore_signal(barrier, inc=1, device_id=device, device_id_type=MESH)

    def lanes(k):
        return pl.ds(pl.multiple_of(k * chunk, chunk), chunk)

    def stage_features(k, carry):
        zbuf[0, k, z] = feat_ref[:, lanes(k)]
        return carry

    lax.fori_loop(0, chunks, stage_features, 0)
    pl.semaphore_wait(barrier, len(peers))

    def send_features(k, carry):
        for d in range(1, nz):
            z_copy(0, k, d, z).start()
        return carry

    lax.fori_loop(0, chunks, send_features, 0)

    count = count_ref[0]
    for t in range(cap):
        pos[t] = jnp.where(t < count, rows_ref[t] * col_tiles + cols_ref[t], -1)

    def place(p, carry):
        slot = jnp.int32(-1)
        for t in range(cap):
            slot = jnp.where(pos[t] == p, jnp.int32(t), slot)
        tile = tiles_ref[jnp.maximum(slot, 0)]
        tile = jnp.where(slot >= 0, tile.astype(F32), 0.0).astype(BF16)
        i, c = p // col_tiles, p % col_tiles
        wout[c % ny, i % 2, c // ny, pl.ds(pl.multiple_of((i // 2) * bt, bt), bt), :] = tile
        return carry

    lax.fori_loop(0, ncol * col_tiles, place, 0)
    for d in range(1, ny):
        w_copy(d, y).start()

    ones = jnp.ones((bt, 128), BF16)

    def row_sum(i, carry):
        total = jnp.zeros((bt, 128), F32)
        for a in range(ny):
            for b in range(nz):
                part = wout[a, i % 2, b, pl.ds(pl.multiple_of((i // 2) * bt, bt), bt), :]
                total += jnp.dot(part, ones, preferred_element_type=F32)
        dsend[i] = total
        return carry

    lax.fori_loop(0, ncol, row_sum, 0)
    for d in range(1, ncol):
        d_copy(d).start()
    wd[y] = wout[y]
    for d in range(1, ny):
        w_copy(d, lax.rem(y - d + ny, ny)).wait_recv()

    def product(it, k, source_y, half):
        total = jnp.zeros((nx * bt, chunk), F32)
        for b in range(nz):
            total += jnp.dot(wd[source_y, half, b], zbuf[it, k, b], preferred_element_type=F32)
        return total.reshape(nx, bt, chunk)

    def multiply(j):
        it, k = j // chunks, j % chunks
        for d in range(1, nz):
            z_copy(it, k, d, lax.rem(z - d + nz, nz)).wait_recv()
        for a in range(ny):
            csend[j, a] = product(it, k, a, 1 - core).astype(BF16)
        c_copy(j).start()
        for a in range(ny):
            keep_c[j % 2, a] = product(it, k, a, core)

    def over_core(j):
        c_copy(j).wait_recv()
        for d in range(1, ny):
            a = lax.rem(y + d, ny)
            ysend[j, d - 1] = (keep_c[j % 2, a] + crecv[j, a].astype(F32)).astype(BF16)
            y_copy(j, d).start()
        keep_y[j % 2] = keep_c[j % 2, y] + crecv[j, y].astype(F32)

    def over_y(j):
        for d in range(1, ny):
            y_copy(j, d).wait_recv()
        for d in range(nx):
            a = lax.rem(x + d, nx)
            total = keep_y[j % 2, a]
            for e in range(1, ny):
                total += yrecv[j, e - 1, a].astype(F32)
            if d == 0:
                keep_x[j % 2] = total
            else:
                xsend[j, d - 1] = total.astype(BF16)
                x_copy(j, d).start()

    def over_x(j):
        it, k = j // chunks, j % chunks

        @pl.when(j == 0)
        def _():
            degree = 1.0 + dsend[col]
            for d in range(1, ncol):
                d_copy(d).wait_recv()
                degree += drecv[d - 1]
            for a in range(chunk // 128):
                scale[:, a * 128:(a + 1) * 128] = RETAIN / degree

        for d in range(1, nx):
            x_copy(j, d).wait_recv()
        total = keep_x[j % 2]
        for d in range(1, nx):
            total += xrecv[j, d - 1].astype(F32)
        source = feat_ref[:, lanes(k)].astype(F32)
        fresh = ((total + zbuf[it, k, z].astype(F32)) * scale[...] + RESTART * source).astype(BF16)

        @pl.when(it == ITERS - 1)
        def _():
            out_ref[:, lanes(k)] = fresh

        @pl.when(it < ITERS - 1)
        def _():
            zbuf[it + 1, k, z] = fresh
            for d in range(1, nz):
                z_copy(it + 1, k, d, z).start()

    def step(s, carry):
        for lag, stage in ((3, over_x), (2, over_y), (1, over_core), (0, multiply)):
            j = s - lag

            @pl.when(jnp.logical_and(j >= 0, j < jobs))
            def _(stage=stage, j=j):
                stage(j)
        return carry

    lax.fori_loop(0, jobs + 3, step, 0)

    def drain(j, carry):
        it, k = j // chunks, j % chunks
        for d in range(1, nz):
            z_copy(it, k, d, z).wait_send()
        c_copy(j).wait_send()
        for d in range(1, ny):
            y_copy(j, d).wait_send()
        for d in range(1, nx):
            x_copy(j, d).wait_send()
        return carry

    lax.fori_loop(0, jobs, drain, 0)
    for d in range(1, ny):
        w_copy(d, y).wait_send()
    for d in range(1, ncol):
        d_copy(d).wait_send()


def body(nz, ny, nx, chunk, features, tile_values, tile_rows, tile_cols, tile_count):
    shard, width = features.shape
    cap, bt = tile_values.shape[2], tile_values.shape[3]
    ncol = nx * 2
    jobs = ITERS * (width // chunk)
    chunks = width // chunk
    dma = pltpu.SemaphoreType.DMA
    smem = pl.BlockSpec(memory_space=pltpu.SMEM)
    vmem = pl.BlockSpec(memory_space=pltpu.VMEM)
    return pl.pallas_call(
        functools.partial(kernel, nz, ny, nx, chunk),
        out_shape=jax.ShapeDtypeStruct((shard, width), BF16),
        in_specs=[vmem, vmem, smem, smem, smem],
        out_specs=vmem,
        scratch_shapes=[
            pltpu.SMEM((cap,), jnp.int32),
            pltpu.VMEM((ny, 2, nz, nx * bt, bt), BF16),
            pltpu.VMEM((ny, 2, nz, nx * bt, bt), BF16),
            pltpu.VMEM((ncol, bt, 128), F32),
            pltpu.VMEM((ncol - 1, bt, 128), F32),
            pltpu.VMEM((bt, chunk), F32),
            pltpu.VMEM((ITERS, chunks, nz, bt, chunk), BF16),
            pltpu.VMEM((jobs, ny, nx, bt, chunk), BF16),
            pltpu.VMEM((jobs, ny, nx, bt, chunk), BF16),
            pltpu.VMEM((2, ny, nx, bt, chunk), F32),
            pltpu.VMEM((jobs, ny - 1, nx, bt, chunk), BF16),
            pltpu.VMEM((jobs, ny - 1, nx, bt, chunk), BF16),
            pltpu.VMEM((2, nx, bt, chunk), F32),
            pltpu.VMEM((jobs, nx - 1, bt, chunk), BF16),
            pltpu.VMEM((jobs, nx - 1, bt, chunk), BF16),
            pltpu.VMEM((2, bt, chunk), F32),
            dma((ny - 1,)), dma((ny - 1,)),
            dma((ncol - 1,)), dma((ncol - 1,)),
            dma((jobs, nz - 1)), dma((jobs, nz - 1)),
            dma((jobs,)), dma((jobs,)),
            dma((jobs, ny - 1)), dma((jobs, ny - 1)),
            dma((jobs, nx - 1)), dma((jobs, nx - 1)),
        ],
        compiler_params=pltpu.CompilerParams(
            collective_id=0, has_side_effects=True, vmem_limit_bytes=62 * 1024 * 1024
        ),
    )(
        features,
        tile_values.reshape(cap, bt, bt),
        tile_rows.reshape(cap),
        tile_cols.reshape(cap),
        tile_count.reshape(1),
    )


def solution(mesh):
    n_row, n_col = mesh.shape["row"], mesh.shape["col"]
    ny = math.isqrt(n_row // 2)
    return jax.shard_map(
        functools.partial(body, n_row // ny, ny, n_col // 2, 128),
        mesh=mesh,
        in_specs=(
            P(("row", "col"), None),
            P("row", "col", None, None, None),
            P("row", "col", None),
            P("row", "col", None),
            P("row", "col"),
        ),
        out_specs=P(("row", "col"), None),
        check_vma=False,
    )
```

```python
import functools
import math

import jax
import jax.numpy as jnp
from jax import lax
from jax.experimental import pallas as pl
from jax.experimental.pallas import tpu as pltpu
from jax.sharding import PartitionSpec as P

ITERS = 2
RETAIN = 0.9
RESTART = 0.1
MESH = pl.DeviceIdType.MESH
F32 = jnp.float32
BF16 = jnp.bfloat16


def kernel(
    nz, ny, nx, chunk,
    feat_ref, tiles_ref, rows_ref, cols_ref, count_ref,
    out_ref,
    pos, wout, wd, dsend, drecv, scale,
    zbuf, csend, crecv, keep_c, ysend, yrecv, keep_y, xsend, xrecv, keep_x,
    w_ss, w_rs, d_ss, d_rs, z_ss, z_rs, c_ss, c_rs, y_ss, y_rs, x_ss, x_rs,
):
    row, col = lax.axis_index("row"), lax.axis_index("col")
    z, y, x, core = row // ny, row % ny, col // 2, col % 2
    ncol = nx * 2
    shard, width = feat_ref.shape
    cap, bt = tiles_ref.shape[0], tiles_ref.shape[1]
    chunks = width // chunk
    jobs = ITERS * chunks
    col_tiles = nz * ny

    def z_peer(d):
        return (lax.rem(z + d, nz) * ny + y, col)

    def y_peer(d):
        return (z * ny + lax.rem(y + d, ny), col)

    def col_peer(d):
        return (row, lax.rem(col + d, ncol))

    def x_peer(d):
        return (row, lax.rem(x + d, nx) * 2 + core)

    sibling = (row, x * 2 + 1 - core)

    def remote(src, dst, ss, rs, device):
        return pltpu.make_async_remote_copy(
            src_ref=src, dst_ref=dst, send_sem=ss, recv_sem=rs, device_id=device, device_id_type=MESH
        )

    def z_copy(it, k, d, owner):
        j = it * chunks + k
        return remote(
            zbuf.at[it, k, owner], zbuf.at[it, k, owner], z_ss.at[j, d - 1], z_rs.at[j, d - 1], z_peer(d)
        )

    def c_copy(j):
        return remote(csend.at[j], crecv.at[j], c_ss.at[j], c_rs.at[j], sibling)

    def y_copy(j, d):
        return remote(ysend.at[j, d - 1], yrecv.at[j, d - 1], y_ss.at[j, d - 1], y_rs.at[j, d - 1], y_peer(d))

    def x_copy(j, d):
        return remote(xsend.at[j, d - 1], xrecv.at[j, d - 1], x_ss.at[j, d - 1], x_rs.at[j, d - 1], x_peer(d))

    def w_copy(d, slot):
        return remote(wout.at[lax.rem(y + d, ny)], wd.at[slot], w_ss.at[d - 1], w_rs.at[d - 1], y_peer(d))

    def d_copy(d):
        return remote(dsend.at[lax.rem(col + d, ncol)], drecv.at[d - 1], d_ss.at[d - 1], d_rs.at[d - 1], col_peer(d))

    barrier = pltpu.get_barrier_semaphore()
    peers = (
        [z_peer(d) for d in range(1, nz)]
        + [y_peer(d) for d in range(1, ny)]
        + [col_peer(d) for d in range(1, ncol)]
    )
    for device in peers:
        pl.semaphore_signal(barrier, inc=1, device_id=device, device_id_type=MESH)

    def lanes(k):
        return pl.ds(pl.multiple_of(k * chunk, chunk), chunk)

    def stage_features(k, carry):
        zbuf[0, k, z] = feat_ref[:, lanes(k)]
        return carry

    lax.fori_loop(0, chunks, stage_features, 0)
    pl.semaphore_wait(barrier, len(peers))

    def send_features(k, carry):
        for d in range(1, nz):
            z_copy(0, k, d, z).start()
        return carry

    lax.fori_loop(0, chunks, send_features, 0)

    count = count_ref[0]
    for t in range(cap):
        pos[t] = jnp.where(t < count, rows_ref[t] * col_tiles + cols_ref[t], -1)

    def place(p, carry):
        slot = jnp.int32(-1)
        for t in range(cap):
            slot = jnp.where(pos[t] == p, jnp.int32(t), slot)
        tile = tiles_ref[jnp.maximum(slot, 0)]
        tile = jnp.where(slot >= 0, tile.astype(F32), 0.0).astype(BF16)
        i, c = p // col_tiles, p % col_tiles
        rows = pl.ds(pl.multiple_of((i // 2) * bt, bt), bt)
        wout[c % ny, i % 2, rows, pl.ds(pl.multiple_of((c // ny) * bt, bt), bt)] = tile
        return carry

    lax.fori_loop(0, ncol * col_tiles, place, 0)
    for d in range(1, ny):
        w_copy(d, y).start()

    ones = jnp.ones((nz * bt, 128), BF16)

    def row_sum(i, carry):
        total = jnp.zeros((bt, 128), F32)
        for a in range(ny):
            part = wout[a, i % 2, pl.ds(pl.multiple_of((i // 2) * bt, bt), bt), :]
            total += jnp.dot(part, ones, preferred_element_type=F32)
        dsend[i] = total
        return carry

    lax.fori_loop(0, ncol, row_sum, 0)
    for d in range(1, ncol):
        d_copy(d).start()
    wd[y] = wout[y]
    for d in range(1, ny):
        w_copy(d, lax.rem(y - d + ny, ny)).wait_recv()

    def product(it, k, source_y, half):
        blocks = zbuf[it, k].reshape(nz * bt, chunk)
        total = jnp.dot(wd[source_y, half], blocks, preferred_element_type=F32)
        return total.reshape(nx, bt, chunk)

    def multiply(j):
        it, k = j // chunks, j % chunks
        for d in range(1, nz):
            z_copy(it, k, d, lax.rem(z - d + nz, nz)).wait_recv()
        for a in range(ny):
            csend[j, :, a] = product(it, k, a, 1 - core).astype(BF16)
        c_copy(j).start()
        for a in range(ny):
            keep_c[j % 2, :, a] = product(it, k, a, core)

    def over_core(j):
        c_copy(j).wait_recv()
        for d in range(1, nx):
            a = lax.rem(x + d, nx)
            xsend[j, d - 1] = (keep_c[j % 2, a] + crecv[j, a].astype(F32)).astype(BF16)
            x_copy(j, d).start()
        keep_x[j % 2] = keep_c[j % 2, x] + crecv[j, x].astype(F32)

    def over_x(j):
        for d in range(1, nx):
            x_copy(j, d).wait_recv()
        for d in range(ny):
            a = lax.rem(y + d, ny)
            total = keep_x[j % 2, a]
            for e in range(1, nx):
                total += xrecv[j, e - 1, a].astype(F32)
            if d == 0:
                keep_y[j % 2] = total
            else:
                ysend[j, d - 1] = total.astype(BF16)
                y_copy(j, d).start()

    def over_y(j):
        it, k = j // chunks, j % chunks

        @pl.when(j == 0)
        def _():
            degree = 1.0 + dsend[col]
            for d in range(1, ncol):
                d_copy(d).wait_recv()
                degree += drecv[d - 1]
            for a in range(chunk // 128):
                scale[:, a * 128:(a + 1) * 128] = RETAIN / degree

        for d in range(1, ny):
            y_copy(j, d).wait_recv()
        total = keep_y[j % 2]
        for d in range(1, ny):
            total += yrecv[j, d - 1].astype(F32)
        source = feat_ref[:, lanes(k)].astype(F32)
        fresh = ((total + zbuf[it, k, z].astype(F32)) * scale[...] + RESTART * source).astype(BF16)

        @pl.when(it == ITERS - 1)
        def _():
            out_ref[:, lanes(k)] = fresh

        @pl.when(it < ITERS - 1)
        def _():
            zbuf[it + 1, k, z] = fresh
            for d in range(1, nz):
                z_copy(it + 1, k, d, z).start()

    def step(s, carry):
        for lag, stage in ((3, over_y), (2, over_x), (1, over_core), (0, multiply)):
            j = s - lag

            @pl.when(jnp.logical_and(j >= 0, j < jobs))
            def _(stage=stage, j=j):
                stage(j)
        return carry

    lax.fori_loop(0, jobs + 3, step, 0)

    def drain(j, carry):
        it, k = j // chunks, j % chunks
        for d in range(1, nz):
            z_copy(it, k, d, z).wait_send()
        c_copy(j).wait_send()
        for d in range(1, ny):
            y_copy(j, d).wait_send()
        for d in range(1, nx):
            x_copy(j, d).wait_send()
        return carry

    lax.fori_loop(0, jobs, drain, 0)
    for d in range(1, ny):
        w_copy(d, y).wait_send()
    for d in range(1, ncol):
        d_copy(d).wait_send()


def body(nz, ny, nx, chunk, features, tile_values, tile_rows, tile_cols, tile_count):
    shard, width = features.shape
    cap, bt = tile_values.shape[2], tile_values.shape[3]
    ncol = nx * 2
    jobs = ITERS * (width // chunk)
    chunks = width // chunk
    dma = pltpu.SemaphoreType.DMA
    smem = pl.BlockSpec(memory_space=pltpu.SMEM)
    vmem = pl.BlockSpec(memory_space=pltpu.VMEM)
    return pl.pallas_call(
        functools.partial(kernel, nz, ny, nx, chunk),
        out_shape=jax.ShapeDtypeStruct((shard, width), BF16),
        in_specs=[vmem, vmem, smem, smem, smem],
        out_specs=vmem,
        scratch_shapes=[
            pltpu.SMEM((cap,), jnp.int32),
            pltpu.VMEM((ny, 2, nx * bt, nz * bt), BF16),
            pltpu.VMEM((ny, 2, nx * bt, nz * bt), BF16),
            pltpu.VMEM((ncol, bt, 128), F32),
            pltpu.VMEM((ncol - 1, bt, 128), F32),
            pltpu.VMEM((bt, chunk), F32),
            pltpu.VMEM((ITERS, chunks, nz, bt, chunk), BF16),
            pltpu.VMEM((jobs, nx, ny, bt, chunk), BF16),
            pltpu.VMEM((jobs, nx, ny, bt, chunk), BF16),
            pltpu.VMEM((2, nx, ny, bt, chunk), F32),
            pltpu.VMEM((jobs, ny - 1, bt, chunk), BF16),
            pltpu.VMEM((jobs, ny - 1, bt, chunk), BF16),
            pltpu.VMEM((2, bt, chunk), F32),
            pltpu.VMEM((jobs, nx - 1, ny, bt, chunk), BF16),
            pltpu.VMEM((jobs, nx - 1, ny, bt, chunk), BF16),
            pltpu.VMEM((2, ny, bt, chunk), F32),
            dma((ny - 1,)), dma((ny - 1,)),
            dma((ncol - 1,)), dma((ncol - 1,)),
            dma((jobs, nz - 1)), dma((jobs, nz - 1)),
            dma((jobs,)), dma((jobs,)),
            dma((jobs, ny - 1)), dma((jobs, ny - 1)),
            dma((jobs, nx - 1)), dma((jobs, nx - 1)),
        ],
        compiler_params=pltpu.CompilerParams(
            collective_id=0, has_side_effects=True, vmem_limit_bytes=62 * 1024 * 1024
        ),
    )(
        features,
        tile_values.reshape(cap, bt, bt),
        tile_rows.reshape(cap),
        tile_cols.reshape(cap),
        tile_count.reshape(1),
    )


def solution(mesh):
    n_row, n_col = mesh.shape["row"], mesh.shape["col"]
    ny = math.isqrt(n_row // 2)
    return jax.shard_map(
        functools.partial(body, n_row // ny, ny, n_col // 2, 256),
        mesh=mesh,
        in_specs=(
            P(("row", "col"), None),
            P("row", "col", None, None, None),
            P("row", "col", None),
            P("row", "col", None),
            P("row", "col"),
        ),
        out_specs=P(("row", "col"), None),
        check_vma=False,
    )
```

```python
import functools
import math

import jax
import jax.numpy as jnp
from jax import lax
from jax.experimental import pallas as pl
from jax.experimental.pallas import tpu as pltpu
from jax.sharding import PartitionSpec as P

ITERS = 2
RETAIN = 0.9
RESTART = 0.1
MESH = pl.DeviceIdType.MESH
F32 = jnp.float32
BF16 = jnp.bfloat16


def kernel(
    nz, ny, nx, chunk,
    feat_ref, tiles_ref, rows_ref, cols_ref, count_ref,
    out_ref,
    pos, wout, wd, dsend, drecv, scale,
    zbuf, csend, crecv, keep_c, ysend, yrecv, keep_y, xsend, xrecv, keep_x,
    w_ss, w_rs, d_ss, d_rs, z_ss, z_rs, c_ss, c_rs, y_ss, y_rs, x_ss, x_rs,
):
    row, col = lax.axis_index("row"), lax.axis_index("col")
    z, y, x, core = row // ny, row % ny, col // 2, col % 2
    ncol = nx * 2
    shard, width = feat_ref.shape
    cap, bt = tiles_ref.shape[0], tiles_ref.shape[1]
    chunks = width // chunk
    jobs = ITERS * chunks
    col_tiles = nz * ny

    def z_peer(d):
        return (lax.rem(z + d, nz) * ny + y, col)

    def y_peer(d):
        return (z * ny + lax.rem(y + d, ny), col)

    def col_peer(d):
        return (row, lax.rem(col + d, ncol))

    def x_peer(d):
        return (row, lax.rem(x + d, nx) * 2 + core)

    sibling = (row, x * 2 + 1 - core)

    def remote(src, dst, ss, rs, device):
        return pltpu.make_async_remote_copy(
            src_ref=src, dst_ref=dst, send_sem=ss, recv_sem=rs, device_id=device, device_id_type=MESH
        )

    def z_copy(it, k, d, owner):
        j = it * chunks + k
        return remote(
            zbuf.at[it, k, owner], zbuf.at[it, k, owner], z_ss.at[j, d - 1], z_rs.at[j, d - 1], z_peer(d)
        )

    def c_copy(j):
        return remote(csend.at[j], crecv.at[j], c_ss.at[j], c_rs.at[j], sibling)

    def y_copy(j, d):
        return remote(ysend.at[j, d - 1], yrecv.at[j, d - 1], y_ss.at[j, d - 1], y_rs.at[j, d - 1], y_peer(d))

    def x_copy(j, d):
        return remote(xsend.at[j, d - 1], xrecv.at[j, d - 1], x_ss.at[j, d - 1], x_rs.at[j, d - 1], x_peer(d))

    def w_copy(d, slot):
        return remote(wout.at[lax.rem(y + d, ny)], wd.at[slot], w_ss.at[d - 1], w_rs.at[d - 1], y_peer(d))

    def d_copy(d):
        return remote(dsend.at[lax.rem(col + d, ncol)], drecv.at[d - 1], d_ss.at[d - 1], d_rs.at[d - 1], col_peer(d))

    barrier = pltpu.get_barrier_semaphore()
    peers = (
        [z_peer(d) for d in range(1, nz)]
        + [y_peer(d) for d in range(1, ny)]
        + [col_peer(d) for d in range(1, ncol)]
    )
    for device in peers:
        pl.semaphore_signal(barrier, inc=1, device_id=device, device_id_type=MESH)

    def lanes(k):
        return pl.ds(pl.multiple_of(k * chunk, chunk), chunk)

    def stage_features(k, carry):
        zbuf[0, k, z] = feat_ref[:, lanes(k)]
        return carry

    lax.fori_loop(0, chunks, stage_features, 0)
    pl.semaphore_wait(barrier, len(peers))

    def send_features(k, carry):
        for d in range(nz - 1, 0, -1):
            z_copy(0, k, d, z).start()
        return carry

    lax.fori_loop(0, chunks, send_features, 0)

    count = count_ref[0]
    for t in range(cap):
        pos[t] = jnp.where(t < count, rows_ref[t] * col_tiles + cols_ref[t], -1)

    def place(p, carry):
        slot = jnp.int32(-1)
        for t in range(cap):
            slot = jnp.where(pos[t] == p, jnp.int32(t), slot)
        tile = tiles_ref[jnp.maximum(slot, 0)]
        tile = jnp.where(slot >= 0, tile.astype(F32), 0.0).astype(BF16)
        i, c = p // col_tiles, p % col_tiles
        rows = pl.ds(pl.multiple_of((i // 2) * bt, bt), bt)
        wout[c % ny, i % 2, rows, pl.ds(pl.multiple_of((c // ny) * bt, bt), bt)] = tile
        return carry

    lax.fori_loop(0, ncol * col_tiles, place, 0)
    for d in range(1, ny):
        w_copy(d, y).start()

    ones = jnp.ones((nz * bt, 128), BF16)

    def row_sum(i, carry):
        total = jnp.zeros((bt, 128), F32)
        for a in range(ny):
            part = wout[a, i % 2, pl.ds(pl.multiple_of((i // 2) * bt, bt), bt), :]
            total += jnp.dot(part, ones, preferred_element_type=F32)
        dsend[i] = total
        return carry

    lax.fori_loop(0, ncol, row_sum, 0)
    for d in range(1, ncol):
        d_copy(d).start()
    wd[y] = wout[y]
    for d in range(1, ny):
        w_copy(d, lax.rem(y - d + ny, ny)).wait_recv()

    def product(it, k, source_y, half):
        blocks = zbuf[it, k].reshape(nz * bt, chunk)
        total = jnp.dot(wd[source_y, half], blocks, preferred_element_type=F32)
        return total.reshape(nx, bt, chunk)

    def multiply(j):
        it, k = j // chunks, j % chunks
        for d in range(1, nz):
            z_copy(it, k, d, lax.rem(z - d + nz, nz)).wait_recv()
        for a in range(ny):
            csend[j, :, a] = product(it, k, a, 1 - core).astype(BF16)
        c_copy(j).start()
        for a in range(ny):
            keep_c[j % 2, :, a] = product(it, k, a, core)

    def over_core(j):
        c_copy(j).wait_recv()
        for d in range(1, nx):
            a = lax.rem(x + d, nx)
            xsend[j, d - 1] = (keep_c[j % 2, a] + crecv[j, a].astype(F32)).astype(BF16)
            x_copy(j, d).start()
        keep_x[j % 2] = keep_c[j % 2, x] + crecv[j, x].astype(F32)

    def over_x(j):
        for d in range(1, nx):
            x_copy(j, d).wait_recv()
        for d in range(ny):
            a = lax.rem(y + d, ny)
            total = keep_x[j % 2, a]
            for e in range(1, nx):
                total += xrecv[j, e - 1, a].astype(F32)
            if d == 0:
                keep_y[j % 2] = total
            else:
                ysend[j, d - 1] = total.astype(BF16)
                y_copy(j, d).start()

    def over_y(j):
        it, k = j // chunks, j % chunks

        @pl.when(j == 0)
        def _():
            degree = 1.0 + dsend[col]
            for d in range(1, ncol):
                d_copy(d).wait_recv()
                degree += drecv[d - 1]
            for a in range(chunk // 128):
                scale[:, a * 128:(a + 1) * 128] = RETAIN / degree

        for d in range(1, ny):
            y_copy(j, d).wait_recv()
        total = keep_y[j % 2]
        for d in range(1, ny):
            total += yrecv[j, d - 1].astype(F32)
        source = feat_ref[:, lanes(k)].astype(F32)
        fresh = ((total + zbuf[it, k, z].astype(F32)) * scale[...] + RESTART * source).astype(BF16)

        @pl.when(it == ITERS - 1)
        def _():
            out_ref[:, lanes(k)] = fresh

        @pl.when(it < ITERS - 1)
        def _():
            zbuf[it + 1, k, z] = fresh
            for d in range(1, nz):
                z_copy(it + 1, k, d, z).start()

    def step(s, carry):
        for lag, stage in ((3, over_y), (2, over_x), (1, over_core), (0, multiply)):
            j = s - lag

            @pl.when(jnp.logical_and(j >= 0, j < jobs))
            def _(stage=stage, j=j):
                stage(j)
        return carry

    lax.fori_loop(0, jobs + 3, step, 0)

    def drain(j, carry):
        it, k = j // chunks, j % chunks
        for d in range(1, nz):
            z_copy(it, k, d, z).wait_send()
        c_copy(j).wait_send()
        for d in range(1, ny):
            y_copy(j, d).wait_send()
        for d in range(1, nx):
            x_copy(j, d).wait_send()
        return carry

    lax.fori_loop(0, jobs, drain, 0)
    for d in range(1, ny):
        w_copy(d, y).wait_send()
    for d in range(1, ncol):
        d_copy(d).wait_send()


def body(nz, ny, nx, chunk, features, tile_values, tile_rows, tile_cols, tile_count):
    shard, width = features.shape
    cap, bt = tile_values.shape[2], tile_values.shape[3]
    ncol = nx * 2
    jobs = ITERS * (width // chunk)
    chunks = width // chunk
    dma = pltpu.SemaphoreType.DMA
    smem = pl.BlockSpec(memory_space=pltpu.SMEM)
    vmem = pl.BlockSpec(memory_space=pltpu.VMEM)
    return pl.pallas_call(
        functools.partial(kernel, nz, ny, nx, chunk),
        out_shape=jax.ShapeDtypeStruct((shard, width), BF16),
        in_specs=[vmem, vmem, smem, smem, smem],
        out_specs=vmem,
        scratch_shapes=[
            pltpu.SMEM((cap,), jnp.int32),
            pltpu.VMEM((ny, 2, nx * bt, nz * bt), BF16),
            pltpu.VMEM((ny, 2, nx * bt, nz * bt), BF16),
            pltpu.VMEM((ncol, bt, 128), F32),
            pltpu.VMEM((ncol - 1, bt, 128), F32),
            pltpu.VMEM((bt, chunk), F32),
            pltpu.VMEM((ITERS, chunks, nz, bt, chunk), BF16),
            pltpu.VMEM((jobs, nx, ny, bt, chunk), BF16),
            pltpu.VMEM((jobs, nx, ny, bt, chunk), BF16),
            pltpu.VMEM((2, nx, ny, bt, chunk), F32),
            pltpu.VMEM((jobs, ny - 1, bt, chunk), BF16),
            pltpu.VMEM((jobs, ny - 1, bt, chunk), BF16),
            pltpu.VMEM((2, bt, chunk), F32),
            pltpu.VMEM((jobs, nx - 1, ny, bt, chunk), BF16),
            pltpu.VMEM((jobs, nx - 1, ny, bt, chunk), BF16),
            pltpu.VMEM((2, ny, bt, chunk), F32),
            dma((ny - 1,)), dma((ny - 1,)),
            dma((ncol - 1,)), dma((ncol - 1,)),
            dma((jobs, nz - 1)), dma((jobs, nz - 1)),
            dma((jobs,)), dma((jobs,)),
            dma((jobs, ny - 1)), dma((jobs, ny - 1)),
            dma((jobs, nx - 1)), dma((jobs, nx - 1)),
        ],
        compiler_params=pltpu.CompilerParams(
            collective_id=0, has_side_effects=True, vmem_limit_bytes=62 * 1024 * 1024
        ),
    )(
        features,
        tile_values.reshape(cap, bt, bt),
        tile_rows.reshape(cap),
        tile_cols.reshape(cap),
        tile_count.reshape(1),
    )


def solution(mesh):
    n_row, n_col = mesh.shape["row"], mesh.shape["col"]
    ny = math.isqrt(n_row // 2)
    return jax.shard_map(
        functools.partial(body, n_row // ny, ny, n_col // 2, 256),
        mesh=mesh,
        in_specs=(
            P(("row", "col"), None),
            P("row", "col", None, None, None),
            P("row", "col", None),
            P("row", "col", None),
            P("row", "col"),
        ),
        out_specs=P(("row", "col"), None),
        check_vma=False,
    )
```

```python
import functools
import math

import jax
import jax.numpy as jnp
from jax import lax
from jax.experimental import pallas as pl
from jax.experimental.pallas import tpu as pltpu
from jax.sharding import PartitionSpec as P

ITERS = 2
RETAIN = 0.9
RESTART = 0.1
MESH = pl.DeviceIdType.MESH
F32 = jnp.float32
BF16 = jnp.bfloat16


def kernel(
    nz, ny, nx, chunk,
    feat_ref, tiles_ref, rows_ref, cols_ref, count_ref,
    out_ref,
    pos, wout, wd, dsend, drecv, scale,
    zbuf, csend, crecv, keep_c, ysend, yrecv, keep_y, xsend, xrecv, keep_x,
    w_ss, w_rs, d_ss, d_rs, z_ss, z_rs, c_ss, c_rs, y_ss, y_rs, x_ss, x_rs,
):
    row, col = lax.axis_index("row"), lax.axis_index("col")
    z, y, x, core = row // ny, row % ny, col // 2, col % 2
    ncol = nx * 2
    shard, width = feat_ref.shape
    cap, bt = tiles_ref.shape[0], tiles_ref.shape[1]
    chunks = width // chunk
    jobs = ITERS * chunks
    col_tiles = nz * ny

    def z_peer(d):
        return (lax.rem(z + d, nz) * ny + y, col)

    def y_peer(d):
        return (z * ny + lax.rem(y + d, ny), col)

    def col_peer(d):
        return (row, lax.rem(col + d, ncol))

    def x_peer(d):
        return (row, lax.rem(x + d, nx) * 2 + core)

    sibling = (row, x * 2 + 1 - core)

    def remote(src, dst, ss, rs, device):
        return pltpu.make_async_remote_copy(
            src_ref=src, dst_ref=dst, send_sem=ss, recv_sem=rs, device_id=device, device_id_type=MESH
        )

    def z_copy(it, k, d, owner):
        j = it * chunks + k
        return remote(
            zbuf.at[it, k, owner], zbuf.at[it, k, owner], z_ss.at[j, d - 1], z_rs.at[j, d - 1], z_peer(d)
        )

    def c_copy(j):
        return remote(csend.at[j], crecv.at[j], c_ss.at[j], c_rs.at[j], sibling)

    def y_copy(j, d):
        return remote(ysend.at[j, d - 1], yrecv.at[j, d - 1], y_ss.at[j, d - 1], y_rs.at[j, d - 1], y_peer(d))

    def x_copy(j, d):
        return remote(xsend.at[j, d - 1], xrecv.at[j, d - 1], x_ss.at[j, d - 1], x_rs.at[j, d - 1], x_peer(d))

    def w_copy(d, slot):
        return remote(wout.at[lax.rem(y + d, ny)], wd.at[slot], w_ss.at[d - 1], w_rs.at[d - 1], y_peer(d))

    def d_copy(d):
        return remote(dsend.at[lax.rem(col + d, ncol)], drecv.at[d - 1], d_ss.at[d - 1], d_rs.at[d - 1], col_peer(d))

    barrier = pltpu.get_barrier_semaphore()
    peers = (
        [z_peer(d) for d in range(1, nz)]
        + [y_peer(d) for d in range(1, ny)]
        + [col_peer(d) for d in range(1, ncol)]
    )
    for device in peers:
        pl.semaphore_signal(barrier, inc=1, device_id=device, device_id_type=MESH)

    def lanes(k):
        return pl.ds(pl.multiple_of(k * chunk, chunk), chunk)

    def stage_features(k, carry):
        zbuf[0, k, z] = feat_ref[:, lanes(k)]
        return carry

    lax.fori_loop(0, chunks, stage_features, 0)
    pl.semaphore_wait(barrier, len(peers))

    def send_features(k, carry):
        for d in range(nz - 1, 0, -1):
            z_copy(0, k, d, z).start()
        return carry

    lax.fori_loop(0, chunks, send_features, 0)

    count = count_ref[0]
    for t in range(cap):
        pos[t] = jnp.where(t < count, rows_ref[t] * col_tiles + cols_ref[t], -1)

    def place(d, q, carry):
        i, c = q // nz, (q % nz) * ny + lax.rem(y + d, ny)
        p = i * col_tiles + c
        slot = jnp.int32(-1)
        for t in range(cap):
            slot = jnp.where(pos[t] == p, jnp.int32(t), slot)
        tile = tiles_ref[jnp.maximum(slot, 0)]
        tile = jnp.where(slot >= 0, tile.astype(F32), 0.0).astype(BF16)
        rows = pl.ds(pl.multiple_of((i // 2) * bt, bt), bt)
        wout[c % ny, i % 2, rows, pl.ds(pl.multiple_of((c // ny) * bt, bt), bt)] = tile
        return carry

    for d in range(1, ny):
        lax.fori_loop(0, ncol * nz, functools.partial(place, d), 0)
        w_copy(d, y).start()
    lax.fori_loop(0, ncol * nz, functools.partial(place, 0), 0)

    ones = jnp.ones((nz * bt, 128), BF16)

    def row_sum(i, carry):
        total = jnp.zeros((bt, 128), F32)
        for a in range(ny):
            part = wout[a, i % 2, pl.ds(pl.multiple_of((i // 2) * bt, bt), bt), :]
            total += jnp.dot(part, ones, preferred_element_type=F32)
        dsend[i] = total
        return carry

    lax.fori_loop(0, ncol, row_sum, 0)
    for d in range(1, ncol):
        d_copy(d).start()
    wd[y] = wout[y]
    for d in range(1, ny):
        w_copy(d, lax.rem(y - d + ny, ny)).wait_recv()

    def product(it, k, source_y, half):
        blocks = zbuf[it, k].reshape(nz * bt, chunk)
        total = jnp.dot(wd[source_y, half], blocks, preferred_element_type=F32)
        return total.reshape(nx, bt, chunk)

    def multiply(j):
        it, k = j // chunks, j % chunks
        for d in range(1, nz):
            z_copy(it, k, d, lax.rem(z - d + nz, nz)).wait_recv()
        for a in range(ny):
            csend[j, :, a] = product(it, k, a, 1 - core).astype(BF16)
        c_copy(j).start()
        for a in range(ny):
            keep_c[j % 2, :, a] = product(it, k, a, core)

    def over_core(j):
        c_copy(j).wait_recv()
        for d in range(1, nx):
            a = lax.rem(x + d, nx)
            xsend[j, d - 1] = (keep_c[j % 2, a] + crecv[j, a].astype(F32)).astype(BF16)
            x_copy(j, d).start()
        keep_x[j % 2] = keep_c[j % 2, x] + crecv[j, x].astype(F32)

    def over_x(j):
        for d in range(1, nx):
            x_copy(j, d).wait_recv()
        for d in range(ny):
            a = lax.rem(y + d, ny)
            total = keep_x[j % 2, a]
            for e in range(1, nx):
                total += xrecv[j, e - 1, a].astype(F32)
            if d == 0:
                keep_y[j % 2] = total
            else:
                ysend[j, d - 1] = total.astype(BF16)
                y_copy(j, d).start()

    def over_y(j):
        it, k = j // chunks, j % chunks

        @pl.when(j == 0)
        def _():
            degree = 1.0 + dsend[col]
            for d in range(1, ncol):
                d_copy(d).wait_recv()
                degree += drecv[d - 1]
            for a in range(chunk // 128):
                scale[:, a * 128:(a + 1) * 128] = RETAIN / degree

        for d in range(1, ny):
            y_copy(j, d).wait_recv()
        total = keep_y[j % 2]
        for d in range(1, ny):
            total += yrecv[j, d - 1].astype(F32)
        source = feat_ref[:, lanes(k)].astype(F32)
        fresh = ((total + zbuf[it, k, z].astype(F32)) * scale[...] + RESTART * source).astype(BF16)

        @pl.when(it == ITERS - 1)
        def _():
            out_ref[:, lanes(k)] = fresh

        @pl.when(it < ITERS - 1)
        def _():
            zbuf[it + 1, k, z] = fresh
            for d in range(1, nz):
                z_copy(it + 1, k, d, z).start()

    def step(s, carry):
        for lag, stage in ((3, over_y), (2, over_x), (1, over_core), (0, multiply)):
            j = s - lag

            @pl.when(jnp.logical_and(j >= 0, j < jobs))
            def _(stage=stage, j=j):
                stage(j)
        return carry

    lax.fori_loop(0, jobs + 3, step, 0)

    def drain(j, carry):
        it, k = j // chunks, j % chunks
        for d in range(1, nz):
            z_copy(it, k, d, z).wait_send()
        c_copy(j).wait_send()
        for d in range(1, ny):
            y_copy(j, d).wait_send()
        for d in range(1, nx):
            x_copy(j, d).wait_send()
        return carry

    lax.fori_loop(0, jobs, drain, 0)
    for d in range(1, ny):
        w_copy(d, y).wait_send()
    for d in range(1, ncol):
        d_copy(d).wait_send()


def body(nz, ny, nx, chunk, features, tile_values, tile_rows, tile_cols, tile_count):
    shard, width = features.shape
    cap, bt = tile_values.shape[2], tile_values.shape[3]
    ncol = nx * 2
    jobs = ITERS * (width // chunk)
    chunks = width // chunk
    dma = pltpu.SemaphoreType.DMA
    smem = pl.BlockSpec(memory_space=pltpu.SMEM)
    vmem = pl.BlockSpec(memory_space=pltpu.VMEM)
    return pl.pallas_call(
        functools.partial(kernel, nz, ny, nx, chunk),
        out_shape=jax.ShapeDtypeStruct((shard, width), BF16),
        in_specs=[vmem, vmem, smem, smem, smem],
        out_specs=vmem,
        scratch_shapes=[
            pltpu.SMEM((cap,), jnp.int32),
            pltpu.VMEM((ny, 2, nx * bt, nz * bt), BF16),
            pltpu.VMEM((ny, 2, nx * bt, nz * bt), BF16),
            pltpu.VMEM((ncol, bt, 128), F32),
            pltpu.VMEM((ncol - 1, bt, 128), F32),
            pltpu.VMEM((bt, chunk), F32),
            pltpu.VMEM((ITERS, chunks, nz, bt, chunk), BF16),
            pltpu.VMEM((jobs, nx, ny, bt, chunk), BF16),
            pltpu.VMEM((jobs, nx, ny, bt, chunk), BF16),
            pltpu.VMEM((2, nx, ny, bt, chunk), F32),
            pltpu.VMEM((jobs, ny - 1, bt, chunk), BF16),
            pltpu.VMEM((jobs, ny - 1, bt, chunk), BF16),
            pltpu.VMEM((2, bt, chunk), F32),
            pltpu.VMEM((jobs, nx - 1, ny, bt, chunk), BF16),
            pltpu.VMEM((jobs, nx - 1, ny, bt, chunk), BF16),
            pltpu.VMEM((2, ny, bt, chunk), F32),
            dma((ny - 1,)), dma((ny - 1,)),
            dma((ncol - 1,)), dma((ncol - 1,)),
            dma((jobs, nz - 1)), dma((jobs, nz - 1)),
            dma((jobs,)), dma((jobs,)),
            dma((jobs, ny - 1)), dma((jobs, ny - 1)),
            dma((jobs, nx - 1)), dma((jobs, nx - 1)),
        ],
        compiler_params=pltpu.CompilerParams(
            collective_id=0, has_side_effects=True, vmem_limit_bytes=62 * 1024 * 1024
        ),
    )(
        features,
        tile_values.reshape(cap, bt, bt),
        tile_rows.reshape(cap),
        tile_cols.reshape(cap),
        tile_count.reshape(1),
    )


def solution(mesh):
    n_row, n_col = mesh.shape["row"], mesh.shape["col"]
    ny = math.isqrt(n_row // 2)
    return jax.shard_map(
        functools.partial(body, n_row // ny, ny, n_col // 2, 256),
        mesh=mesh,
        in_specs=(
            P(("row", "col"), None),
            P("row", "col", None, None, None),
            P("row", "col", None),
            P("row", "col", None),
            P("row", "col"),
        ),
        out_specs=P(("row", "col"), None),
        check_vma=False,
    )
```
